32 devices in a mesh: rep: 1, ep: 32 (over z, y, x, core).
Axes of the slice: x: 2, y: 2, z: 4, core: 2. Of those that a mesh axis runs over, the one named last changes fastest.
Arguments:
- tokens: bfloat16 [2560, 3584], P(('rep', 'ep')), may hold values from -6 to 6
- norm_gain: bfloat16 [3584], replicated, may hold values from 0.099609375 to 1.8984375
- routes: int32 [2560, 8], P(('rep', 'ep')), may hold values from 0 to 63, all different within a row; in each aligned block of 80 rows (0 to 79, 80 to 159, ...) at most 11 rows name the same one
- gate_weights: float32 [2560, 8], P(('rep', 'ep')), may hold values from 0.05 to 0.5
- up_codes: int32 [64, 512, 1024], P('ep'), may hold values from 0 to 16368
- up_levels: bfloat16 [64, 4, 1024], P('ep'), may hold values from -0.09375 to 0.09375
- down_codes: int32 [64, 1024, 512], P('ep'), may hold values from 0 to 16368
- down_levels: bfloat16 [64, 4, 3584], P('ep'), may hold values from -0.1875 to 0.1875
Outputs:
- layer_output: bfloat16 [2560, 3584], P(('rep', 'ep'))
The draws below stay inside these ranges and needn't reach their ends.
Inputs may be any that keep to these rules, and one draw needn't show every extreme that they name: `routes`: each row names 8 different experts. Among the 80 rows of one device no expert is named by more than 11 rows, a bound that some block reaches.
All inputs are finite; a program needn't handle non-finite values.
Results may differ from the reference program's by a relative error of at most 0.0051.
Values may be sent and summed in bfloat16 or wider, within the bound.
A program may use at most 128 MiB of HBM per device.

```python
import math
import jax
import jax.numpy as jnp
import numpy as np
from jax import lax

D = 3584
FF = 1024
TOP = 8
TOK_DEV = 80
EXPERTS = 64
TOKENS = 2560
CAP = 11
N_EP = 32


def place_ends(array, key, smallest, largest):
    index_at = [jax.random.randint(jax.random.fold_in(key, axis), (), 0, length) for axis, length in enumerate(array.shape)]
    widest = array.shape.index(max(array.shape))
    beside = index_at[:widest] + [(index_at[widest] + 1) % array.shape[widest]] + index_at[widest + 1:]
    return array.at[tuple(index_at)].set(smallest).at[tuple(beside)].set(largest)


def block_scale(key, shape, split, low, top_value):
    gain = 1.0
    for dim, shards_of in split:
        steps = jax.random.uniform(jax.random.fold_in(jax.random.fold_in(key, 6), dim), (shards_of,), jnp.float32, low / len(split), top_value / len(split))
        gain = gain * jnp.repeat(jnp.exp(steps), shape[dim] // shards_of).reshape((-1,) + (1,) * (len(shape) - 1 - dim))
    return gain


def shared_out(key, own, number, rows, number_of, top, bound, lean):
    order = jax.random.permutation(key, number_of)
    crowded, common = portions_of(number_of, rows * top, bound, lean, True), portions_of(number_of, rows * top, bound, lean, False)
    places = jnp.arange(number_of)

    def named(tallies, turn):
        used = int((tallies > 0).sum())
        fixed = max(1, used // 4)
        shifted = fixed + (places - fixed + turn * (used - fixed)) % max(1, number_of - fixed)
        return jnp.zeros((number_of,), jnp.int32).at[order[jnp.where(places < fixed, places, shifted)]].set(jnp.asarray(tallies, jnp.int32))

    tallies = jnp.where(number % 4 == 0, named(crowded, number // 4), named(common, number - number // 4 - 1))
    mixed = jax.random.permutation(jax.random.fold_in(own, 3), number_of)
    giver, taker = mixed[0:number_of // 2 * 2:2], mixed[1:number_of // 2 * 2:2]
    margin = jnp.minimum(tallies[giver] - 1, bound - tallies[taker]) // 2
    margin = jnp.where((giver == order[0]) | (taker == order[0]) | (tallies[taker] == 0), 0, jnp.maximum(margin, 0))
    shifted = jax.random.randint(jax.random.fold_in(own, 4), (number_of // 2,), 0, 1 << 20) % (margin + 1)
    tallies = tallies.at[giver].add(-shifted).at[taker].add(shifted)
    members = jnp.searchsorted(jnp.cumsum(tallies), jnp.arange(rows * top), side="right").astype(jnp.int32)
    listing = members.reshape(top, rows).T
    listing = listing[jax.random.permutation(jax.random.fold_in(own, 1), rows)]
    turn = jax.random.randint(jax.random.fold_in(own, 2), (rows, 1), 0, top)
    return jnp.take_along_axis(listing, (jnp.arange(top)[None, :] + turn) % top, axis=1)


def portions_of(number_of, total, reach, lean, full):
    portions = [(1 << 20) // math.isqrt(standing ** lean) + 1 for standing in range(1, number_of + 1)]
    largest = reach if full else min(reach, max(-(-total // number_of), total * portions[0] // sum(portions)))
    least = 1 if total - largest >= number_of - 1 else 0
    given, surplus = [largest] + [least] * (number_of - 1), total - largest - least * (number_of - 1)
    while surplus > 0:
        movable = [i for i in range(1, number_of) if given[i] < largest] or [i for i in range(1, number_of) if given[i] < reach]
        pool, remaining = sum([portions[i] for i in movable]), surplus
        for i in movable:
            addition = min(reach - given[i], max(1, remaining * portions[i] // pool), surplus)
            given[i] = given[i] + addition
            surplus = surplus - addition
    return np.array(given)


def gaussian(own_key, shape, scale, most, shards=(), held_as=jnp.bfloat16):
    array = scale * jax.random.normal(own_key, shape, jnp.float32)
    if shards:
        array = array * block_scale(own_key, shape, shards, -0.22, 0.18)
    return jnp.clip(array, -most, most).astype(held_as)


def setup_inputs(seed: int = 0, part: int = 0) -> dict:
    keys = jax.random.split(jax.random.key(seed), 9)
    part_splits = jax.random.split(jax.random.fold_in(keys[8], part), 9)
    tokens = gaussian(part_splits[0], (TOKENS, D), 1.0, 6.0, ((0, 32),))
    norm_gain = jnp.clip(1.0 + 0.18 * jax.random.normal(keys[1], (D,), jnp.float32), 0.099609375, 1.8984375).astype(jnp.bfloat16)
    routes_keys = jax.random.split(jax.random.fold_in(part_splits[2], 1), TOKENS // TOK_DEV)
    routes_turns = jax.random.permutation(jax.random.fold_in(part_splits[2], 3), TOKENS // TOK_DEV)
    routes = jax.vmap(lambda own, number: shared_out(jax.random.fold_in(part_splits[2], 2), own, number, TOK_DEV, EXPERTS, TOP, CAP, 2))(routes_keys, routes_turns).reshape((TOKENS, TOP))
    gate_weights = jnp.clip(jnp.exp(math.log(0.5) - 2.3025851 * jax.random.uniform(part_splits[3], (TOKENS, TOP), jnp.float32) ** block_scale(part_splits[3], (TOKENS, TOP), ((0, 32),), -0.2, 0.2)), 0.05, 0.5)
    up_codes = place_ends(jax.random.randint(keys[4], (EXPERTS, D // 7, FF), 0, 16369), jax.random.fold_in(keys[4], 1), 0, 16368).astype(jnp.int32)
    up_levels = gaussian(keys[5], (EXPERTS, 4, FF), D ** -0.5, 0.09375, ((0, 32),))
    down_codes = place_ends(jax.random.randint(keys[6], (EXPERTS, FF, D // 7), 0, 16369), jax.random.fold_in(keys[6], 1), 0, 16368).astype(jnp.int32)
    down_levels = gaussian(keys[7], (EXPERTS, 4, D), FF ** -0.5, 0.1875, ((0, 32),))
    return {"tokens": tokens, "norm_gain": norm_gain, "routes": routes, "gate_weights": gate_weights, "up_codes": up_codes, "up_levels": up_levels, "down_codes": down_codes, "down_levels": down_levels}


def pick_level(picked, level_zero, level_one, level_two, level_three):
    return jnp.where(picked == 0, level_zero, jnp.where(picked == 1, level_one, jnp.where(picked == 2, level_two, level_three)))

def expand_rows(packed, levels):
    shift_bits = 2 * jnp.arange(7, dtype=jnp.int32)
    picked = jnp.bitwise_and(jnp.right_shift(packed[..., :, None, :], shift_bits[:, None]), 3)
    tables = [levels[..., k, :][..., None, None, :] for k in range(4)]
    result = pick_level(picked, tables[0], tables[1], tables[2], tables[3])
    shape = result.shape
    return result.reshape(shape[:-3] + (shape[-3] * 7, shape[-1]))

def expand_columns(packed, levels):
    shift_bits = 2 * jnp.arange(7, dtype=jnp.int32)
    picked = jnp.bitwise_and(jnp.right_shift(packed[..., None], shift_bits), 3)
    grouped = levels.reshape(levels.shape[:-1] + (levels.shape[-1] // 7, 7))
    tables = [grouped[..., k, :, :][..., None, :, :] for k in range(4)]
    result = pick_level(picked, tables[0], tables[1], tables[2], tables[3])
    shape = result.shape
    return result.reshape(shape[:-2] + (shape[-2] * 7,))

def reference(tokens, norm_gain, routes, gate_weights, up_codes, up_levels, down_codes, down_levels):
    wide = tokens.astype(jnp.float32)
    scale = lax.rsqrt(lax.optimization_barrier(jnp.mean(wide * wide, axis=-1, keepdims=True)) + 1e-06)
    normed = (wide * scale * norm_gain.astype(jnp.float32)).astype(jnp.bfloat16)
    flat_routes = routes.reshape(-1)
    flat_gates = gate_weights.reshape(-1)
    slot_bound = N_EP * CAP

    def one_expert(total, pieces):
        expert_id, up_packed, up_table, down_packed, down_table = pieces
        chosen = flat_routes == expert_id
        positions = jnp.nonzero(chosen, size=slot_bound, fill_value=0)[0].astype(jnp.int32)
        is_live = (jnp.arange(slot_bound) < jnp.sum(chosen.astype(jnp.int32))).astype(jnp.float32)
        token_rows = (positions // TOP).astype(jnp.int32)
        inputs = normed[token_rows]
        hidden = jax.nn.silu(jnp.dot(inputs, expand_rows(up_packed, up_table), preferred_element_type=jnp.float32)).astype(jnp.bfloat16)
        outputs = jnp.dot(hidden, expand_columns(down_packed, down_table), preferred_element_type=jnp.float32).astype(jnp.bfloat16)
        weight = flat_gates[positions] * is_live
        total = total.at[token_rows].add(outputs.astype(jnp.float32) * weight[:, None])
        return (total, None)
    start = jnp.zeros((TOKENS, D), jnp.float32)
    routed, _ = lax.scan(one_expert, start, (jnp.arange(EXPERTS, dtype=jnp.int32), up_codes, up_levels, down_codes, down_levels))
    return routed.astype(jnp.bfloat16)
```

```python
import functools

import jax
import jax.numpy as jnp
from jax import lax
from jax.experimental import pallas as pl
from jax.experimental.pallas import tpu as pltpu
from jax.sharding import PartitionSpec as P

DIGITS = 7
LANES = 128
F32 = jnp.float32
BF16 = jnp.bfloat16


def kernel(
    inner, outer, cap, slots,
    tok_ref, gain_ref, meta_ref, uc_hbm, ul_ref, dc_hbm, dl_ref,
    out_ref,
    meta, xz, gathered, arrived, returned, zsend, zrecv, pown, pbuf,
    uc, dc, perm, perm_t, pick, spread, spread_hi, spread_lo, levels, weight, acc, hidden,
    load_sem, meta_s, meta_r, z_s, z_r, p_s, p_r, q_s, q_r, y_s, y_r,
):
    me = lax.axis_index("ep")
    mz = me // inner
    mp = me % inner
    tok, features = tok_ref.shape
    experts, words, hid = uc.shape
    plane = inner * experts
    rows = experts * slots
    blocks = words // LANES
    wide_block = DIGITS * LANES

    load_up = pltpu.make_async_copy(uc_hbm, uc, load_sem.at[0])
    load_down = pltpu.make_async_copy(dc_hbm, dc, load_sem.at[1])
    load_up.start()
    load_down.start()

    def column(o):
        return {"ep": ((mz + o) % outer) * inner + mp}

    def group(o):
        return {"ep": mz * inner + (mp + o) % inner}

    barrier = pltpu.get_barrier_semaphore()
    for o in range(1, outer):
        pl.semaphore_signal(barrier, inc=1, device_id=column(o), device_id_type=pl.DeviceIdType.MESH)
    for o in range(1, inner):
        pl.semaphore_signal(barrier, inc=1, device_id=group(o), device_id_type=pl.DeviceIdType.MESH)

    def remote(src, dst, send, recv, device):
        return pltpu.make_async_remote_copy(
            src_ref=src, dst_ref=dst, send_sem=send, recv_sem=recv,
            device_id=device, device_id_type=pl.DeviceIdType.MESH,
        )

    def meta_copy(o):
        return remote(meta.at[mz], meta.at[mz], meta_s.at[o], meta_r.at[o], column(o))

    def z_copy(d, o):
        mine = xz.at[d, mz, pl.ds(0, tok)]
        return remote(mine, mine, z_s.at[d, o], z_r.at[d, o], column(o))

    def p_copy(d, o):
        return remote(gathered.at[d, (mp + o) % inner], arrived.at[d, mp], p_s.at[d, o], p_r.at[d, o], group(o))

    def q_copy(d, o):
        return remote(gathered.at[d, (mp + o) % inner], returned.at[d, mp], q_s.at[d, o], q_r.at[d, o], group(o))

    def y_copy(d, o):
        return remote(zsend.at[d, (mz + o) % outer], zrecv.at[d, o], y_s.at[d, o], y_r.at[d, o], column(o))

    r = lax.broadcasted_iota(jnp.int32, (wide_block, wide_block), 0)
    c = lax.broadcasted_iota(jnp.int32, (wide_block, wide_block), 1)
    perm[...] = jnp.where(r == DIGITS * (c & (LANES - 1)) + (c >> 7), 1.0, 0.0).astype(BF16)

    wide = tok_ref[...].astype(F32)
    scale = lax.rsqrt(jnp.mean(wide * wide, axis=-1, keepdims=True) + 1e-06)
    normed = (wide * scale * gain_ref[...].astype(F32)).astype(BF16)
    meta[mz] = meta_ref[...]
    for w in range(blocks):
        part = jnp.dot(normed[:, w * wide_block:(w + 1) * wide_block], perm[...], preferred_element_type=F32).astype(BF16)
        for d in range(DIGITS):
            xz[d, mz, 0:tok, w * LANES:(w + 1) * LANES] = part[:, d * LANES:(d + 1) * LANES]

    pl.semaphore_wait(barrier, outer + inner - 2)
    for o in range(1, outer):
        meta_copy(o).start()

    def send_z(d, carry):
        for o in range(1, outer):
            z_copy(d, o).start()
        return carry

    lax.fori_loop(0, DIGITS, send_z, 0)

    tall = xz.shape[2]
    for d in range(DIGITS):
        xz[d, :, tok:tall, :] = jnp.zeros((outer, tall - tok, words), BF16)
    perm_t[...] = jnp.where(c == DIGITS * (r & (LANES - 1)) + (r >> 7), 1.0, 0.0).astype(BF16)
    for w in range(blocks):
        part = jnp.dot(dl_ref[:, w * wide_block:(w + 1) * wide_block], perm[...], preferred_element_type=F32)
        for d in range(DIGITS):
            levels[d, :, w * LANES:(w + 1) * LANES] = part[:, d * LANES:(d + 1) * LANES]

    before = jnp.where(
        lax.broadcasted_iota(jnp.int32, (tall, tall), 0) < lax.broadcasted_iota(jnp.int32, (tall, tall), 1), 1.0, 0.0
    ).astype(BF16)
    for o in range(1, outer):
        meta_copy(o).wait_recv()
    ids = (lax.broadcasted_iota(jnp.int32, (plane, tall), 0) + mz * plane).astype(F32)
    place = lax.broadcasted_iota(jnp.int32, (slots, tall), 0).astype(F32)
    top = meta.shape[1] // 2
    for b in range(outer):
        named = jnp.zeros((plane, tall), F32)
        gate = jnp.zeros((plane, tall), F32)
        for k in range(top):
            hit = meta[b, k:k + 1, :] == ids
            named = named + jnp.where(hit, 1.0, 0.0)
            gate = gate + jnp.where(hit, meta[b, top + k:top + k + 1, :], 0.0)
        rank = jnp.dot(named.astype(BF16), before, preferred_element_type=F32)
        slot = jnp.where(named > 0.5, rank + float(b * cap), -1.0)
        for e in range(plane):
            here = place == slot[e:e + 1, :]
            pick[e * slots:(e + 1) * slots, b * tall:(b + 1) * tall] = jnp.where(here, 1.0, 0.0).astype(BF16)
            spread[e * slots:(e + 1) * slots, :] = jnp.where(here, gate[e:e + 1, :], 0.0)
        turned = spread[...].T
        high = turned.astype(BF16)
        spread_hi[b * tall:(b + 1) * tall, :] = high
        spread_lo[b * tall:(b + 1) * tall, :] = (turned - high.astype(F32)).astype(BF16)

    def relay(d, carry):
        for o in range(1, outer):
            z_copy(d, o).wait_recv()
        tokens = xz[d].reshape(outer * tall, words)
        chosen = jnp.dot(pick[...], tokens, preferred_element_type=F32).astype(BF16)
        gathered[d] = chosen.reshape(inner, rows, words)
        for o in range(1, inner):
            p_copy(d, o).start()
        arrived[d, mp] = gathered[d, mp]
        return carry

    lax.fori_loop(0, DIGITS, relay, 0)

    def unpack(codes, j, d, tables, depth, width):
        low = jnp.left_shift(jnp.int32(1), 2 * d)
        high = jnp.left_shift(jnp.int32(2), 2 * d)
        for t in range(0, width, min(256, width)):
            stop = min(t + 256, width)
            zero, one, two, three = (table[:, t:stop] for table in tables)

            def piece(i, carry):
                at = pl.ds(pl.multiple_of(i * 64, 64), 64)
                word = codes[j, at, t:stop]
                odd = (word & low) != 0
                upper = (word & high) != 0
                value = jnp.where(upper, jnp.where(odd, three, two), jnp.where(odd, one, zero))
                weight[at, t:stop] = value.astype(BF16)
                return carry

            lax.fori_loop(0, depth // 64, piece, 0, unroll=2)

    load_up.wait()
    acc[...] = jnp.zeros_like(acc)

    def up(d, carry):
        for o in range(1, inner):
            p_copy(d, o).wait_recv()
        for j in range(experts):
            tables = [ul_ref[j, k:k + 1, :].astype(F32) for k in range(4)]
            unpack(uc, j, d, tables, words, hid)
            x = arrived[d, :, j * slots:(j + 1) * slots, :].reshape(inner * slots, words)
            acc[j] = acc[j] + jnp.dot(x, weight[0:words, 0:hid], preferred_element_type=F32)
        return carry

    lax.fori_loop(0, DIGITS, up, 0)
    for j in range(experts):
        v = acc[j]
        hidden[j] = (v / (1.0 + jnp.exp(-v))).astype(BF16)

    load_down.wait()

    def sent(d, carry):
        for o in range(1, inner):
            p_copy(d, o).wait_send()
        return carry

    lax.fori_loop(0, DIGITS, sent, 0)
    answer = gathered

    def down(d, carry):
        for j in range(experts):
            tables = [levels[d, j * 4 + k:j * 4 + k + 1, :] for k in range(4)]
            unpack(dc, j, d, tables, hid, words)
            y = jnp.dot(hidden[j], weight[0:hid, 0:words], preferred_element_type=F32).astype(BF16)
            answer[d, :, j * slots:(j + 1) * slots, :] = y.reshape(inner, slots, words)
        for o in range(1, inner):
            q_copy(d, o).start()
        returned[d, mp] = answer[d, mp]
        return carry

    lax.fori_loop(0, DIGITS, down, 0)

    def combine(d, carry):
        for o in range(1, inner):
            q_copy(d, o).wait_recv()
        y = returned[d].reshape(inner * rows, words)
        total = jnp.dot(spread_hi[...], y, preferred_element_type=F32) + jnp.dot(
            spread_lo[...], y, preferred_element_type=F32
        )
        pbuf[...] = total.reshape(outer, tall, words)
        zsend[d] = pbuf[:, 0:tok, :].astype(BF16)
        for o in range(1, outer):
            y_copy(d, o).start()
        pown[d] = pbuf[mz, 0:tok, :]
        return carry

    lax.fori_loop(0, DIGITS, combine, 0)

    def finish(d, carry):
        for o in range(1, outer):
            y_copy(d, o).wait_recv()
        total = pown[d]
        for o in range(1, outer):
            total = total + zrecv[d, o].astype(F32)
        pown[d] = total
        return carry

    lax.fori_loop(0, DIGITS, finish, 0)
    for w in range(blocks):
        line = jnp.concatenate([pown[d, :, w * LANES:(w + 1) * LANES] for d in range(DIGITS)], axis=1).astype(BF16)
        out_ref[:, w * wide_block:(w + 1) * wide_block] = jnp.dot(
            line, perm_t[...], preferred_element_type=F32
        ).astype(BF16)

    for o in range(1, outer):
        meta_copy(o).wait_send()

    def drain(d, carry):
        for o in range(1, outer):
            z_copy(d, o).wait_send()
            y_copy(d, o).wait_send()
        for o in range(1, inner):
            q_copy(d, o).wait_send()
        return carry

    lax.fori_loop(0, DIGITS, drain, 0)


def body(inner, tokens, norm_gain, routes, gate_weights, up_codes, up_levels, down_codes, down_levels):
    tok, features = tokens.shape
    top = routes.shape[1]
    experts, words, hid = up_codes.shape
    peers = lax.axis_size("ep")
    outer = peers // inner
    cap = max(2, tok * top // (experts * peers) + 1)
    slots = -(-outer * cap // 16) * 16
    tall = LANES
    rows = experts * slots
    meta = jnp.concatenate([routes.astype(F32), gate_weights], axis=1).T
    meta = jnp.pad(meta, ((0, 0), (0, tall - tok)), constant_values=-1.0)
    vmem = pl.BlockSpec(memory_space=pltpu.VMEM)
    hbm = pl.BlockSpec(memory_space=pl.ANY)
    per_group = (DIGITS, inner, rows, words)
    dma = pltpu.SemaphoreType.DMA
    return pl.pallas_call(
        functools.partial(kernel, inner, outer, cap, slots),
        out_shape=jax.ShapeDtypeStruct((tok, features), BF16),
        in_specs=[vmem, vmem, vmem, hbm, vmem, hbm, vmem],
        out_specs=vmem,
        scratch_shapes=[
            pltpu.VMEM((outer, 2 * top, tall), F32),
            pltpu.VMEM((DIGITS, outer, tall, words), BF16),
            pltpu.VMEM(per_group, BF16),
            pltpu.VMEM(per_group, BF16),
            pltpu.VMEM(per_group, BF16),
            pltpu.VMEM((DIGITS, outer, tok, words), BF16),
            pltpu.VMEM((DIGITS, outer, tok, words), BF16),
            pltpu.VMEM((DIGITS, tok, words), F32),
            pltpu.VMEM((outer, tall, words), F32),
            pltpu.VMEM(up_codes.shape, jnp.int32),
            pltpu.VMEM(down_codes.shape, jnp.int32),
            pltpu.VMEM((DIGITS * LANES, DIGITS * LANES), BF16),
            pltpu.VMEM((DIGITS * LANES, DIGITS * LANES), BF16),
            pltpu.VMEM((inner * rows, outer * tall), BF16),
            pltpu.VMEM((inner * rows, tall), F32),
            pltpu.VMEM((outer * tall, inner * rows), BF16),
            pltpu.VMEM((outer * tall, inner * rows), BF16),
            pltpu.VMEM((DIGITS, experts * 4, words), F32),
            pltpu.VMEM((max(words, hid), max(words, hid)), BF16),
            pltpu.VMEM((experts, inner * slots, hid), F32),
            pltpu.VMEM((experts, inner * slots, hid), BF16),
            dma((2,)),
            dma((outer,)), dma((outer,)),
            dma((DIGITS, outer)), dma((DIGITS, outer)),
            dma((DIGITS, inner)), dma((DIGITS, inner)),
            dma((DIGITS, inner)), dma((DIGITS, inner)),
            dma((DIGITS, outer)), dma((DIGITS, outer)),
        ],
        compiler_params=pltpu.CompilerParams(
            collective_id=0, has_side_effects=True, vmem_limit_bytes=63 * 1024 * 1024
        ),
    )(
        tokens, norm_gain.reshape(1, features), meta, up_codes, up_levels, down_codes,
        down_levels.reshape(experts * 4, features),
    )


def solution(mesh):
    peers = mesh.shape["ep"]
    inner = 8 if peers % 8 == 0 and peers > 8 else max(1, peers // 2)
    placed = (
        P(("rep", "ep"), None),
        P(),
        P(("rep", "ep"), None),
        P(("rep", "ep"), None),
        P("ep", None, None),
        P("ep", None, None),
        P("ep", None, None),
        P("ep", None, None),
    )
    return jax.shard_map(
        functools.partial(body, inner), mesh=mesh, in_specs=placed, out_specs=P(("rep", "ep"), None), check_vma=False
    )
```
